768 devices in a mesh: fsdp: 96 (over z, y), grp: 8 (over x, core).
Axes of the slice: x: 4, y: 8, z: 12, core: 2. Of those that a mesh axis runs over, the one named last changes fastest.
Arguments:
- grad_shards: bfloat16 [75497472], P(('fsdp', 'grp')), may hold values from -0.3984375 to 0.3984375
- shard_length: int32 [768], replicated, may hold values from 32768 to 98304, as said below
- block_owner: int32 [192], replicated, may hold values from 0 to 767, as said below
- left_factor: bfloat16 [768, 512, 512], P(('fsdp', 'grp'))
- right_factor: bfloat16 [768, 512, 512], P(('fsdp', 'grp'))
- left_root: bfloat16 [768, 512, 512], P(('fsdp', 'grp'))
- right_root: bfloat16 [768, 512, 512], P(('fsdp', 'grp'))
Outputs:
- direction_shards: bfloat16 [75497472], P(('fsdp', 'grp'))
- new_left: bfloat16 [768, 512, 512], P(('fsdp', 'grp'))
- new_right: bfloat16 [768, 512, 512], P(('fsdp', 'grp'))
The draws below stay inside these ranges and needn't reach their ends.
Inputs may be any that keep to these rules, and one draw needn't show every extreme that they name: shard_length[d] = 65536 + u_d - u_(d-1) with integers -16384 <= u_d <= 16384, u_(-1) = 0 and the last u = 0, so device d's shard ends at (d+1) * 65536 + u_d. `block_owner`: block k is owned by one of the devices 4 * k to 4 * k + 4 - 1 (devices numbered fsdp-major); a device owns at most one block.
All inputs are finite; a program needn't handle non-finite values.
Results may differ from the reference program's by a relative error of at most 0.0049.
Values may be sent and summed in bfloat16 or wider, within the bound.
A program may use at most 64 MiB of HBM per device.

```python
import jax
import jax.numpy as jnp
from jax import lax

B = 512
BLOCK_SHARDS = 4
SHARD = 65536
CAP = 98304
NBLK = 192
DEVICES = 768


def factor_like(key, lowest, highest, spread):
    first_key, second_key = jax.random.split(key)
    count = NBLK * BLOCK_SHARDS
    noise = spread * jax.random.normal(first_key, (count, B, B), jnp.float32)
    diag_values = jnp.exp(jax.random.uniform(second_key, (count, B, 1), jnp.float32, jnp.log(lowest), jnp.log(highest)))
    marks = jnp.arange(B, dtype=jnp.int32)
    identity = (marks[:, None] == marks[None, :]).astype(jnp.float32)
    return noise + identity[None] * diag_values


def draw_shard_length(key, part):
    key = jax.random.fold_in(key, 11)
    jitter = SHARD // 4
    count = NBLK * BLOCK_SHARDS
    shifts = jax.random.randint(key, (count,), -jitter, jitter + 1).astype(jnp.int32)
    marks = jnp.arange(count, dtype=jnp.int32)
    shifts = jnp.where(marks == 0, -jitter, shifts)
    shifts = jnp.where(marks == 1, jitter, shifts)
    shifts = jnp.where(marks == 2, jitter, shifts)
    shifts = jnp.where(marks == 3, -jitter, shifts)
    shifts = jnp.where(marks == count - 1, 0, shifts)
    before = jnp.concatenate([jnp.zeros((1,), jnp.int32), shifts[:-1]])
    return (SHARD + shifts - before).astype(jnp.int32)


def draw_block_owner(key, part):
    key = jax.random.fold_in(key, 13)
    marks = jnp.arange(NBLK, dtype=jnp.int32)
    picks = jax.random.randint(key, (NBLK,), 0, BLOCK_SHARDS).astype(jnp.int32)
    picks = jnp.where(marks == 0, 0, picks)
    picks = jnp.where(marks == NBLK - 1, BLOCK_SHARDS - 1, picks)
    return (marks * BLOCK_SHARDS + picks).astype(jnp.int32)


def draw_left_factor(key, part):
    key = jax.random.fold_in(key, 21)
    return factor_like(key, 0.5, 3.0, 0.02).astype(jnp.bfloat16)


def draw_right_factor(key, part):
    key = jax.random.fold_in(key, 23)
    return factor_like(key, 0.5, 3.0, 0.02).astype(jnp.bfloat16)


def draw_left_root(key, part):
    key = jax.random.fold_in(key, 25)
    return factor_like(key, 1.0, 6.0, 0.04).astype(jnp.bfloat16)


def draw_right_root(key, part):
    key = jax.random.fold_in(key, 27)
    return factor_like(key, 1.0, 6.0, 0.04).astype(jnp.bfloat16)


def levels(rng, dims, cuts, smallest, high):
    gain = 1.0
    for axis_at, blocks in cuts:
        heights = jax.random.uniform(jax.random.fold_in(jax.random.fold_in(rng, 6), axis_at), (blocks,), jnp.float32, smallest / len(cuts), high / len(cuts))
        gain = gain * jnp.repeat(jnp.exp(heights), dims[axis_at] // blocks).reshape((-1,) + (1,) * (len(dims) - 1 - axis_at))
    return gain


def centred(rng, extent, width, limit, cuts=(), held_as=jnp.bfloat16):
    factor_of = levels(rng, extent, cuts, -0.22, 0.18) if cuts else 1.0
    array = jax.random.normal(rng, extent, jnp.float32) * width * factor_of
    return jnp.minimum(jnp.maximum(array, -limit), limit).astype(held_as)


def setup_inputs(seed: int = 0) -> dict:
    seeds = jax.random.split(jax.random.key(seed), 8)
    return {
        "grad_shards": centred(seeds[0], (DEVICES * CAP,), 0.05, 0.3984375, ((0, 768),)),
        "shard_length": draw_shard_length(jax.random.fold_in(seeds[7], 71), 0),
        "block_owner": draw_block_owner(jax.random.fold_in(seeds[7], 71), 0),
        "left_factor": draw_left_factor(jax.random.fold_in(seeds[7], 71), 0),
        "right_factor": draw_right_factor(jax.random.fold_in(seeds[7], 71), 0),
        "left_root": draw_left_root(jax.random.fold_in(seeds[7], 71), 0),
        "right_root": draw_right_root(jax.random.fold_in(seeds[7], 71), 0),
    }


def update_block(items):
    grad_block, left_old, right_old, left_inv, right_inv = items
    gram_left = jnp.einsum("ik,jk->ij", grad_block.astype(jnp.float32), grad_block.astype(jnp.float32))
    gram_right = jnp.einsum("ki,kj->ij", grad_block.astype(jnp.float32), grad_block.astype(jnp.float32))
    fresh_left = (0.9 * left_old.astype(jnp.float32) + 0.1 * gram_left).astype(jnp.bfloat16)
    fresh_right = (0.9 * right_old.astype(jnp.float32) + 0.1 * gram_right).astype(jnp.bfloat16)
    halfway = jnp.dot(left_inv, grad_block, preferred_element_type=jnp.float32).astype(jnp.bfloat16)
    precond = jnp.dot(halfway, right_inv, preferred_element_type=jnp.float32).astype(jnp.bfloat16)
    return fresh_left, fresh_right, precond


def reference(grad_shards, shard_length, block_owner, left_factor, right_factor, left_root, right_root):
    devices = shard_length.shape[0]
    offsets = (jnp.cumsum(shard_length, dtype=jnp.int32) - shard_length).astype(jnp.int32)
    total = NBLK * B * B
    places = jnp.arange(total, dtype=jnp.int32)
    holder = (jnp.searchsorted(offsets, places, side="right").astype(jnp.int32) - 1).astype(jnp.int32)
    source = (holder * CAP + (places - offsets[holder])).astype(jnp.int32)
    blocks = grad_shards[source].reshape(NBLK, B, B)
    fresh_left, fresh_right, precond = lax.map(update_block, (blocks, left_factor[block_owner], right_factor[block_owner], left_root[block_owner], right_root[block_owner]))
    new_left = jnp.zeros((devices, B, B), jnp.bfloat16).at[block_owner].set(fresh_left)
    new_right = jnp.zeros((devices, B, B), jnp.bfloat16).at[block_owner].set(fresh_right)
    direction_shards = jnp.zeros((devices * CAP,), jnp.bfloat16).at[source].set(precond.reshape(total))
    return direction_shards, new_left, new_right
```

```python
import functools

import jax
import jax.numpy as jnp
from jax import lax
from jax.experimental import pallas as pl
from jax.experimental.pallas import tpu as pltpu
from jax.sharding import PartitionSpec as P

B = 512
LANES = 128
PART = 128
EDGE = 32
WROWS = PART + 2 * EDGE
REST = PART - EDGE
FLAT = WROWS * B // LANES
SPLIT = B // LANES
PAD = 264
MESH = pl.DeviceIdType.MESH

NEAR_ROWS = 80
LAST = 64
OUTER_ROWS = 2 * NEAR_ROWS
THEIR_ROWS = 2 * PART + EDGE

LEFT, RIGHT, SIB, PREV, NEXT, ACROSS = 0, 1, 2, 4, 5, 6

(
    R_EDGES, R_MAIN, R_PART, R_SEAM, R_ACROSS, R_PREV, R_NEXT, R_FWD, R_LROOT, R_RROOT, R_SOON, R_LAST,
    R_BACK, R_HEAD, R_HELLO, R_THEIRS, R_PASSED, RECVS,
) = (0, 1, 2, 4, 6, 7, 8, 9, 13, 14, 15, 17, 19, 20, 22, 23, 25, 27)
SENDS = 30


def kernel(
    lens_hbm, owner_hbm, grad_hbm, lfac_hbm, rfac_hbm, lroot_hbm, rroot_hbm,
    dir_out, nl_out, nr_out,
    lens, owner, grad, shifted, edges, main, block, lroot, rroot, picked, ltheirs, rtheirs, lfac, rfac,
    pout, pown, pin, head_out, head_in, hello, zwin,
    in_sem, send_sem, recv_sem,
):
    f = lax.axis_index("fsdp")
    g = lax.axis_index("grp")
    nf = lax.axis_size("fsdp")
    ng = lax.axis_size("grp")
    me = f * ng + g
    part = g % 4
    core = g % 2
    chip = part // 2
    first = (3 - part) // 3
    final = part // 3
    outer = first + final
    inner = 1 - outer
    base = me - part
    has_prev = base > 0
    has_next = base + 4 < nf * ng
    is_outer = outer == 1
    is_inner = inner == 1
    gives = jnp.logical_and(base == 0, chip == 1)
    takes = jnp.logical_and(base == 0, chip == 0)
    sends_rows = jnp.logical_not(gives)
    gets_rows = jnp.logical_not(takes)
    gives_inner = jnp.logical_and(is_inner, gives)
    gives_outer = jnp.logical_and(is_outer, gives)
    takes_inner = jnp.logical_and(is_inner, takes)
    takes_outer = jnp.logical_and(is_outer, takes)
    gets_inner = jnp.logical_and(is_inner, gets_rows)
    gets_outer = jnp.logical_and(is_outer, gets_rows)
    beyond = jnp.logical_or(jnp.logical_and(chip == 0, has_prev), jnp.logical_and(chip == 1, has_next))
    outer_beyond = jnp.logical_and(is_outer, beyond)
    inner_prev = jnp.logical_and(is_inner, has_prev)
    inner_next = jnp.logical_and(is_inner, has_next)

    def device(index):
        index = index + ng
        return index // ng - 1, index % ng

    sib = (f, g + 1 - 2 * core)
    land = (f, g - part + 2 - chip)
    diag = (f, g - part + 3 - 3 * chip)
    sib_part = part + 1 - 2 * core
    other = 2 - 2 * chip

    def only(there, act):
        if there is None:
            act()
        else:
            pl.when(there)(act)

    def spot(start, size):
        return pl.ds(pl.multiple_of(start, 16), size)

    loads = []

    def load(src, dst):
        copy = pltpu.make_async_copy(src, dst, in_sem.at[len(loads)])
        copy.start()
        loads.append(copy)
        return copy

    sends = []

    def send(src, dst, to, arrival, there=None):
        copy = pltpu.make_async_remote_copy(
            src_ref=src,
            dst_ref=dst,
            send_sem=send_sem.at[len(sends)],
            recv_sem=recv_sem.at[arrival],
            device_id=to,
            device_id_type=MESH,
        )
        only(there, copy.start)
        sends.append((copy, there))
        return len(sends) - 1

    def sent(index):
        copy, there = sends[index]
        sends[index] = None
        only(there, copy.wait_send)

    def arrived(dst, arrival, here=None):
        copy = pltpu.make_async_remote_copy(
            src_ref=dst,
            dst_ref=dst,
            send_sem=send_sem.at[0],
            recv_sem=recv_sem.at[arrival],
            device_id=sib,
            device_id_type=MESH,
        )
        only(here, copy.wait_recv)

    load_grad = load(grad_hbm, grad)
    load_lens = load(lens_hbm, lens)

    barrier = pltpu.get_barrier_semaphore()
    for to, there in (
        (sib, is_inner),
        (land, is_inner),
        (diag, is_inner),
        (device(base - 1), inner_prev),
        (device(base + 4), inner_next),
        (device(base - 3 + 8 * chip), outer_beyond),
        (device(base - 2 + 8 * chip), outer_beyond),
    ):
        only(there, functools.partial(pl.semaphore_signal, barrier, 1, device_id=to, device_id_type=MESH))
    greetings = inner * (1 + has_prev.astype(jnp.int32) + has_next.astype(jnp.int32)) + outer * (
        2 + 2 * beyond.astype(jnp.int32)
    )

    def meet():
        pl.semaphore_wait(barrier, greetings)

    hello[0] = jnp.zeros(hello.shape[1:], hello.dtype)
    pl.when(is_outer)(meet)
    send(hello.at[0], hello.at[1], sib, R_HELLO, is_outer)
    send(lroot_hbm.at[0], lroot.at[1], sib, R_LROOT, is_outer)
    send(rroot_hbm.at[0], rroot.at[1], sib, R_RROOT, is_outer)

    load_owner = load(owner_hbm, owner)
    load_roots = [load(lroot_hbm.at[0], lroot.at[0]), load(rroot_hbm.at[0], rroot.at[0])]
    load_facs = [load(lfac_hbm.at[0], lfac), load(rfac_hbm.at[0], rfac)]

    load_lens.wait()
    counts = lens[...] - PART * B
    spots = lax.broadcasted_iota(jnp.int32, counts.shape, 0) * counts.shape[1] + lax.broadcasted_iota(
        jnp.int32, counts.shape, 1
    )

    def shift_of(index):
        return jnp.sum(jnp.where(spots < index, counts, 0))

    own_shift = shift_of(me)
    next_shift = shift_of(me + 1)
    start = jnp.clip(own_shift + EDGE * B, 0, 2 * EDGE * B)
    length = next_shift - own_shift + PART * B
    down = start // LANES
    along = start % LANES

    load_grad.wait()
    chunk = FLAT // 8
    for i in range(8):
        at = i * chunk
        shifted[pl.ds(PAD + at, chunk), :] = pltpu.roll(
            grad[pl.ds(at, chunk), :].astype(jnp.float32), along, 1
        )

    def window(row, size, *dsts):
        lane = lax.broadcasted_iota(jnp.int32, (size, LANES), 1)
        for j in range(SPLIT):
            here = shifted[pl.ds(PAD - down + row * SPLIT + j, size, stride=SPLIT), :]
            above = shifted[pl.ds(PAD - 1 - down + row * SPLIT + j, size, stride=SPLIT), :]
            value = jnp.where(lane < along, above, here).astype(jnp.bfloat16)
            for dst in dsts:
                dst[:, pl.ds(j * LANES, LANES)] = value

    window(0, EDGE, edges.at[LEFT])
    window(WROWS - EDGE, EDGE, edges.at[RIGHT])
    window(EDGE, PART, main, block.at[spot(part * PART, PART)])

    pl.when(is_inner)(meet)

    rest = core * EDGE
    send(main.at[spot(rest, REST)], block.at[spot(part * PART + rest, REST)], land, R_PART + core)
    send(edges.at[1 - chip], edges.at[ACROSS], land, R_ACROSS, is_inner)
    for i in (1, 2):
        send(edges.at[chip], edges.at[NEXT - chip], device(base - 4 + 8 * chip + i), R_NEXT - chip, outer_beyond)
    arrived(hello.at[1], R_HELLO, is_inner)
    send(edges.at[pl.ds(LEFT, 2)], edges.at[pl.ds(SIB, 2)], sib, R_EDGES)
    send(main, block.at[spot(part * PART, PART)], sib, R_MAIN)
    send(lroot_hbm.at[0], lroot.at[1], sib, R_LROOT, is_inner)
    send(rroot_hbm.at[0], rroot.at[1], sib, R_RROOT, is_inner)

    lines = lax.broadcasted_iota(jnp.int32, (EDGE, B), 0) * B + lax.broadcasted_iota(jnp.int32, (EDGE, B), 1)

    def merge(row, bound, slot, before):
        rows = spot(row, EDGE)
        here = block[rows, :].astype(jnp.float32)
        there = edges[slot].astype(jnp.float32)
        place = lines + row * B
        keep = place < bound if before else place >= bound
        block[rows, :] = jnp.where(keep, here, there).astype(jnp.bfloat16)

    pieces = (
        spot(other * PART, REST),
        spot(other * PART + PART + EDGE, REST),
        spot(other * PART + PART - EDGE, 2 * EDGE),
    )
    forwards = []

    def pass_on(there, prev_there, next_there):
        for i in range(2):
            arrived(block.at[pieces[i]], R_PART + i, there)
            forwards.append(send(block.at[pieces[i]], block.at[pieces[i]], sib, R_FWD + i, there))
        for i in range(2):
            rows = spot(other * PART + PART - EDGE + EDGE * i, EDGE)
            arrived(block.at[rows], R_SEAM + i, there)
        send(block.at[pieces[2]], block.at[pieces[2]], sib, R_FWD + 2, there)
        arrived(edges.at[ACROSS], R_ACROSS, there)
        arrived(edges.at[PREV], R_PREV, prev_there)
        arrived(edges.at[NEXT], R_NEXT, next_there)
        send(edges.at[pl.ds(PREV, 3)], edges.at[pl.ds(PREV, 3)], sib, R_FWD + 3, there)

    pass_on(takes_inner, jnp.logical_and(takes_inner, has_prev), jnp.logical_and(takes_inner, has_next))

    seam = 2 * chip * PART + PART
    seam_bound = seam * B + jnp.where(core == 0, next_shift, own_shift)
    arrived(edges.at[pl.ds(SIB, 2)], R_EDGES)
    arrived(block.at[spot(sib_part * PART, PART)], R_MAIN)
    merge(seam - EDGE, seam_bound, LEFT + SIB * (1 - core), True)
    merge(seam, seam_bound, RIGHT + SIB * core, False)
    seam_rows = spot(seam - EDGE + EDGE * core, EDGE)
    send(block.at[seam_rows], block.at[seam_rows], land, R_SEAM + core)

    load_owner.wait()
    owner_part = owner[me // 4] - base
    slot = jnp.where(owner_part == part, 0, 1)
    near = owner_part // 2 == chip
    owns = owner_part == part
    for copy in load_roots:
        copy.wait()
    arrived(lroot.at[1], R_LROOT, gives)
    arrived(rroot.at[1], R_RROOT, gives)

    @pl.when(gives_inner)
    def _():
        picked[...] = rroot[slot]

    @pl.when(gives_outer)
    def _():
        picked[pl.ds(0, THEIR_ROWS), :] = lroot[slot, pl.ds(0, THEIR_ROWS), :]

    send(picked, rtheirs, land, R_THEIRS, gives_inner)
    send(picked.at[pl.ds(0, THEIR_ROWS)], ltheirs, land, R_THEIRS + 1, gives_outer)

    bounds = [PART * B * j + shift_of(base + j) for j in (0, 2, 4)]

    pass_on(gets_inner, jnp.logical_and(gets_inner, has_prev), jnp.logical_and(gets_inner, has_next))
    for index in forwards:
        sent(index)
    for i in range(3):
        arrived(block.at[pieces[i]], R_FWD + i, is_outer)
    arrived(edges.at[pl.ds(PREV, 3)], R_FWD + 3, is_outer)

    merge(0, bounds[0], PREV, False)
    merge(2 * PART - EDGE, bounds[1], ACROSS - (ACROSS - SIB * core) * chip, True)
    merge(2 * PART, bounds[1], ACROSS - (ACROSS - RIGHT - SIB * (1 - core)) * (1 - chip), False)
    merge(4 * PART - EDGE, bounds[2], NEXT, True)

    arrived(lroot.at[1], R_LROOT, sends_rows)
    arrived(rroot.at[1], R_RROOT, sends_rows)

    def direction(*rows):
        lines = [lroot[slot, spot(row, size), :] for row, size in rows]
        left = lines[0] if len(lines) == 1 else jnp.concatenate(lines, axis=0)
        half = jnp.dot(left, block[...], preferred_element_type=jnp.float32).astype(jnp.bfloat16)
        return jnp.dot(half, rroot[slot], preferred_element_type=jnp.float32).astype(jnp.bfloat16)

    soon = (1 - chip) * (4 * PART - 2 * NEAR_ROWS + NEAR_ROWS * outer) + chip * NEAR_ROWS * inner
    last = (1 - chip) * (2 * PART - EDGE + LAST * outer) + chip * (2 * NEAR_ROWS + LAST * inner)

    @pl.when(is_inner)
    def _():
        ends = direction((0, EDGE), (4 * PART - EDGE, EDGE))
        head_out[0] = ends[:EDGE]
        head_out[1] = ends[EDGE:]

    send(head_out.at[0], head_in.at[chip], device(base - 1), R_HEAD + chip, inner_prev)
    send(head_out.at[1], head_in.at[chip], device(base + 4), R_HEAD + chip, inner_next)

    @pl.when(sends_rows)
    def _():
        pout[pl.ds(0, NEAR_ROWS), :] = direction((soon, NEAR_ROWS))

    send(pout.at[pl.ds(0, NEAR_ROWS)], pin.at[spot(soon, NEAR_ROWS)], land, R_SOON + core, sends_rows)

    @pl.when(sends_rows)
    def _():
        pout[pl.ds(NEAR_ROWS, LAST), :] = direction((last, LAST))

    send(pout.at[pl.ds(NEAR_ROWS, LAST)], pin.at[spot(last, LAST)], land, R_LAST + core, sends_rows)

    mine_at = part * PART - EDGE + EDGE * first - EDGE * final
    pown[...] = direction((mine_at, WROWS))

    for copy in load_facs:
        copy.wait()
    for dst, fac, dims in ((nl_out, lfac, (1, 1)), (nr_out, rfac, (0, 0))):
        for i in range(SPLIT):
            strip = pl.ds(i * LANES, LANES)
            one = block[strip, :] if dims[0] == 1 else block[:, strip]
            gram = lax.dot_general(
                one,
                block[...],
                (((dims[0],), (dims[1],)), ((), ())),
                preferred_element_type=jnp.float32,
            )
            fresh = 0.9 * fac[strip, :].astype(jnp.float32) + 0.1 * gram
            dst[0, strip, :] = jnp.where(owns, fresh, 0.0).astype(jnp.bfloat16)

    def sender_rows(whose):
        outer_there = (whose + chip) % 2
        near_at = chip * (4 * PART - 2 * NEAR_ROWS + NEAR_ROWS * outer_there) + (1 - chip) * NEAR_ROWS * (
            1 - outer_there
        )
        last_at = chip * (2 * PART - EDGE + LAST * outer_there) + (1 - chip) * (
            2 * NEAR_ROWS + LAST * (1 - outer_there)
        )
        return near_at, last_at

    for i in range(2):
        near_at, _ = sender_rows(i)
        arrived(pin.at[spot(near_at, NEAR_ROWS)], R_SOON + i, gets_inner)
    outer_rows = spot(chip * (4 * PART - OUTER_ROWS), OUTER_ROWS)
    send(pin.at[outer_rows], pin.at[outer_rows], sib, R_BACK, gets_inner)
    for i in range(2):
        _, last_at = sender_rows(i)
        arrived(pin.at[spot(last_at, LAST)], R_LAST + i, gets_inner)
    arrived(pin.at[outer_rows], R_BACK, gets_outer)
    for i, ref in ((1, ltheirs), (0, rtheirs)):
        arrived(ref, R_THEIRS + i, takes_inner)
        send(ref, ref, sib, R_PASSED + i, takes_inner)
        arrived(ref, R_PASSED + i, takes_outer)

    @pl.when(takes)
    def _():
        left = ltheirs[spot(part * (PART - EDGE), WROWS), :]
        half = jnp.dot(left, block[...], preferred_element_type=jnp.float32).astype(jnp.bfloat16)
        pin[spot(part * (PART - EDGE), WROWS), :] = jnp.dot(
            half, rtheirs[...], preferred_element_type=jnp.float32
        ).astype(jnp.bfloat16)


    def mine(at, row, size):
        return jnp.where(
            near,
            pown[spot(at, size), :].astype(jnp.float32),
            pin[spot(row, size), :].astype(jnp.float32),
        )

    def place(row, value):
        for j in range(SPLIT):
            zwin[pl.ds(row * SPLIT + j, value.shape[0], stride=SPLIT), :] = pltpu.roll(
                value[:, j * LANES : (j + 1) * LANES], (LANES - along) % LANES, 1
            )

    place(EDGE, mine(EDGE - EDGE * first + EDGE * final, part * PART, PART))
    for i in range(2):
        arrived(head_in.at[i], R_HEAD + i, outer_beyond)
    beside = jnp.clip(me // 4 - 1 + 2 * chip, 0, owner.shape[0] - 1)
    head = jnp.where(
        (owner[beside] - 4 * beside) // 2 == 0,
        head_in[0].astype(jnp.float32),
        head_in[1].astype(jnp.float32),
    )
    top = mine(EDGE * final, part * PART - EDGE + EDGE * first, EDGE)
    place(0, jnp.where(part == 0, head, top))
    bottom = mine(EDGE + PART - EDGE * first, part * PART + PART - EDGE * final, EDGE)
    place(EDGE + PART, jnp.where(part == 3, head, bottom))

    lane = lax.broadcasted_iota(jnp.int32, (chunk, LANES), 1)
    flat = lax.broadcasted_iota(jnp.int32, (chunk, LANES), 0) * LANES + lane
    for i in range(8):
        at = i * chunk
        here = zwin[pl.ds(down + at, chunk), :]
        below = zwin[pl.ds(down + at + 1, chunk), :]
        value = jnp.where(lane + along < LANES, here, below)
        value = jnp.where(flat + at * LANES < length, value, 0.0)
        dir_out[pl.ds(at, chunk), :] = value.astype(jnp.bfloat16)

    for pair in sends:
        if pair is not None:
            only(pair[1], pair[0].wait_send)


def hand_over(*refs):
    sem = refs[-1]
    copies = [pltpu.make_async_copy(refs[i], refs[3 + i], sem.at[i]) for i in range(3)]
    for copy in copies:
        copy.start()
    for copy in copies:
        copy.wait()


def local(grad_shards, shard_length, block_owner, left_factor, right_factor, left_root, right_root):
    count = shard_length.shape[0]
    wide = LANES if count % LANES == 0 else count
    bf16 = jnp.bfloat16
    square = jax.ShapeDtypeStruct((1, B, B), bf16)
    call = pl.pallas_call(
        kernel,
        out_shape=(
            pltpu.VMEM((FLAT, LANES), bf16), pltpu.VMEM((1, B, B), bf16), pltpu.VMEM((1, B, B), bf16)
        ),
        in_specs=[pl.BlockSpec(memory_space=pl.ANY)] * 7,
        out_specs=[pl.BlockSpec(memory_space=pltpu.VMEM)] * 3,
        scratch_shapes=[
            pltpu.VMEM((count // wide, wide), jnp.int32),
            pltpu.SMEM(block_owner.shape, jnp.int32),
            pltpu.VMEM((FLAT, LANES), bf16),
            pltpu.VMEM((PAD + FLAT, LANES), jnp.float32),
            pltpu.VMEM((7, EDGE, B), bf16),
            pltpu.VMEM((PART, B), bf16),
            pltpu.VMEM((B, B), bf16),
            pltpu.VMEM((2, B, B), bf16),
            pltpu.VMEM((2, B, B), bf16),
            pltpu.VMEM((B, B), bf16),
            pltpu.VMEM((THEIR_ROWS, B), bf16),
            pltpu.VMEM((B, B), bf16),
            pltpu.VMEM((B, B), bf16),
            pltpu.VMEM((B, B), bf16),
            pltpu.VMEM((NEAR_ROWS + LAST, B), bf16),
            pltpu.VMEM((WROWS, B), bf16),
            pltpu.VMEM((B, B), bf16),
            pltpu.VMEM((2, EDGE, B), bf16),
            pltpu.VMEM((2, EDGE, B), bf16),
            pltpu.VMEM((2, 16, LANES), bf16),
            pltpu.VMEM((FLAT + PAD, LANES), jnp.float32),
            pltpu.SemaphoreType.DMA((7,)),
            pltpu.SemaphoreType.DMA((SENDS,)),
            pltpu.SemaphoreType.DMA((RECVS,)),
        ],
        compiler_params=pltpu.CompilerParams(
            collective_id=0, has_side_effects=True, vmem_limit_bytes=48 * 1024 * 1024
        ),
        name="shampoo_step",
    )
    given = (
        shard_length.reshape(count // wide, wide),
        block_owner,
        grad_shards.reshape(FLAT, LANES),
        left_factor,
        right_factor,
        left_root,
        right_root,
    )
    results = call(*(pltpu.with_memory_space_constraint(x, pltpu.HBM) for x in given))
    direction, new_left, new_right = pl.pallas_call(
        hand_over,
        out_shape=(jax.ShapeDtypeStruct((FLAT, LANES), bf16), square, square),
        in_specs=[pl.BlockSpec(memory_space=pltpu.VMEM)] * 3,
        out_specs=[pl.BlockSpec(memory_space=pl.ANY)] * 3,
        scratch_shapes=[pltpu.SemaphoreType.DMA((3,))],
        compiler_params=pltpu.CompilerParams(vmem_limit_bytes=16 * 1024 * 1024),
        name="hand_over",
    )(*(pltpu.with_memory_space_constraint(x, pltpu.VMEM) for x in results))
    return direction.reshape(grad_shards.shape), new_left, new_right


def solution(mesh):
    flat = P(("fsdp", "grp"))
    square = P(("fsdp", "grp"), None, None)
    return jax.shard_map(
        local,
        mesh=mesh,
        in_specs=(flat, P(), P(), square, square, square, square),
        out_specs=(flat, square, square),
        check_vma=False,
    )
```

```python
import functools

import jax
import jax.numpy as jnp
from jax import lax
from jax.experimental import pallas as pl
from jax.experimental.pallas import tpu as pltpu
from jax.sharding import PartitionSpec as P

B = 512
LANES = 128
PART = 128
EDGE = 32
WROWS = PART + 2 * EDGE
REST = PART - EDGE
FLAT = WROWS * B // LANES
SPLIT = B // LANES
PAD = 264
MESH = pl.DeviceIdType.MESH

NEAR_ROWS = 80
LAST = 64
OUTER_ROWS = 2 * NEAR_ROWS
THEIR_ROWS = 2 * PART + EDGE

LEFT, RIGHT, SIB, PREV, NEXT, ACROSS = 0, 1, 2, 4, 5, 6

(
    R_EDGES, R_MAIN, R_PART, R_SEAM, R_ACROSS, R_PREV, R_NEXT, R_FWD, R_LROOT, R_RROOT, R_SOON, R_LAST,
    R_BACK, R_HEAD, R_HELLO, R_THEIRS, R_PASSED, RECVS,
) = (0, 1, 2, 4, 6, 7, 8, 9, 13, 14, 15, 17, 19, 20, 22, 23, 25, 27)
SENDS = 30


def kernel(
    lens_hbm, owner_hbm, grad_hbm, lfac_hbm, rfac_hbm, lroot_hbm, rroot_hbm,
    dir_out, nl_out, nr_out,
    lens, owner, grad, shifted, edges, main, block, lroot, rroot, picked, ltheirs, rtheirs, lfac, rfac,
    pout, pown, pin, head_out, head_in, hello, halfway, zwin,
    in_sem, send_sem, recv_sem,
):
    f = lax.axis_index("fsdp")
    g = lax.axis_index("grp")
    nf = lax.axis_size("fsdp")
    ng = lax.axis_size("grp")
    me = f * ng + g
    part = g % 4
    core = g % 2
    chip = part // 2
    first = (3 - part) // 3
    final = part // 3
    outer = first + final
    inner = 1 - outer
    base = me - part
    has_prev = base > 0
    has_next = base + 4 < nf * ng
    is_outer = outer == 1
    is_inner = inner == 1
    gives = jnp.logical_and(base == 0, chip == 1)
    takes = jnp.logical_and(base == 0, chip == 0)
    sends_rows = jnp.logical_not(gives)
    gets_rows = jnp.logical_not(takes)
    greets_sib = jnp.logical_or(is_inner, gets_rows)
    early_roots = jnp.logical_and(is_outer, base == 0)
    gives_inner = jnp.logical_and(is_inner, gives)
    gives_outer = jnp.logical_and(is_outer, gives)
    takes_inner = jnp.logical_and(is_inner, takes)
    takes_outer = jnp.logical_and(is_outer, takes)
    gets_inner = jnp.logical_and(is_inner, gets_rows)
    gets_outer = jnp.logical_and(is_outer, gets_rows)
    beyond = jnp.logical_or(jnp.logical_and(chip == 0, has_prev), jnp.logical_and(chip == 1, has_next))
    outer_beyond = jnp.logical_and(is_outer, beyond)
    inner_prev = jnp.logical_and(is_inner, has_prev)
    inner_next = jnp.logical_and(is_inner, has_next)

    def device(index):
        index = index + ng
        return index // ng - 1, index % ng

    sib = (f, g + 1 - 2 * core)
    land = (f, g - part + 2 - chip)
    diag = (f, g - part + 3 - 3 * chip)
    sib_part = part + 1 - 2 * core
    other = 2 - 2 * chip

    def only(there, act):
        if there is None:
            act()
        else:
            pl.when(there)(act)

    def spot(start, size):
        return pl.ds(pl.multiple_of(start, 16), size)

    loads = []

    def load(src, dst):
        copy = pltpu.make_async_copy(src, dst, in_sem.at[len(loads)])
        copy.start()
        loads.append(copy)
        return copy

    sends = []

    def send(src, dst, to, arrival, there=None):
        copy = pltpu.make_async_remote_copy(
            src_ref=src,
            dst_ref=dst,
            send_sem=send_sem.at[len(sends)],
            recv_sem=recv_sem.at[arrival],
            device_id=to,
            device_id_type=MESH,
        )
        only(there, copy.start)
        sends.append((copy, there))
        return len(sends) - 1

    def sent(index):
        copy, there = sends[index]
        sends[index] = None
        only(there, copy.wait_send)

    def arrived(dst, arrival, here=None):
        copy = pltpu.make_async_remote_copy(
            src_ref=dst,
            dst_ref=dst,
            send_sem=send_sem.at[0],
            recv_sem=recv_sem.at[arrival],
            device_id=sib,
            device_id_type=MESH,
        )
        only(here, copy.wait_recv)

    load_grad = load(grad_hbm, grad)
    load_lens = load(lens_hbm, lens)

    barrier = pltpu.get_barrier_semaphore()
    for to, there in (
        (sib, greets_sib),
        (land, is_inner),
        (diag, is_inner),
        (device(base - 1), inner_prev),
        (device(base + 4), inner_next),
        (device(base - 3 + 8 * chip), outer_beyond),
        (device(base - 2 + 8 * chip), outer_beyond),
    ):
        only(there, functools.partial(pl.semaphore_signal, barrier, 1, device_id=to, device_id_type=MESH))
    greetings = inner * (1 + gets_rows.astype(jnp.int32) + has_prev.astype(jnp.int32) + has_next.astype(jnp.int32)) + outer * (
        2 + 2 * beyond.astype(jnp.int32)
    )

    def meet():
        pl.semaphore_wait(barrier, greetings)

    hello[0] = jnp.zeros(hello.shape[1:], hello.dtype)
    pl.when(is_outer)(meet)
    send(hello.at[0], hello.at[1], sib, R_HELLO, takes_outer)
    send(lroot_hbm.at[0], lroot.at[1], sib, R_LROOT, early_roots)
    send(rroot_hbm.at[0], rroot.at[1], sib, R_RROOT, early_roots)

    load_owner = load(owner_hbm, owner)
    load_roots = [load(lroot_hbm.at[0], lroot.at[0]), load(rroot_hbm.at[0], rroot.at[0])]
    load_facs = [load(lfac_hbm.at[0], lfac), load(rfac_hbm.at[0], rfac)]

    load_lens.wait()
    counts = lens[...] - PART * B
    spots = lax.broadcasted_iota(jnp.int32, counts.shape, 0) * counts.shape[1] + lax.broadcasted_iota(
        jnp.int32, counts.shape, 1
    )

    def shift_of(index):
        return jnp.sum(jnp.where(spots < index, counts, 0))

    own_shift = shift_of(me)
    next_shift = shift_of(me + 1)
    start = jnp.clip(own_shift + EDGE * B, 0, 2 * EDGE * B)
    length = next_shift - own_shift + PART * B
    down = start // LANES
    along = start % LANES

    load_grad.wait()
    chunk = FLAT // 8
    for i in range(8):
        at = i * chunk
        shifted[pl.ds(PAD + at, chunk), :] = pltpu.roll(
            grad[pl.ds(at, chunk), :].astype(jnp.float32), along, 1
        )

    def window(row, size, *dsts):
        lane = lax.broadcasted_iota(jnp.int32, (size, LANES), 1)
        for j in range(SPLIT):
            here = shifted[pl.ds(PAD - down + row * SPLIT + j, size, stride=SPLIT), :]
            above = shifted[pl.ds(PAD - 1 - down + row * SPLIT + j, size, stride=SPLIT), :]
            value = jnp.where(lane < along, above, here).astype(jnp.bfloat16)
            for dst in dsts:
                dst[:, pl.ds(j * LANES, LANES)] = value

    window(0, EDGE, edges.at[LEFT])
    window(WROWS - EDGE, EDGE, edges.at[RIGHT])
    window(EDGE, PART, main, block.at[spot(part * PART, PART)])

    pl.when(is_inner)(meet)

    rest = core * EDGE
    send(main.at[spot(rest, REST)], block.at[spot(part * PART + rest, REST)], land, R_PART + core)
    send(edges.at[1 - chip], edges.at[ACROSS], land, R_ACROSS, is_inner)
    for i in (1, 2):
        send(edges.at[chip], edges.at[NEXT - chip], device(base - 4 + 8 * chip + i), R_NEXT - chip, outer_beyond)
    arrived(hello.at[1], R_HELLO, takes_inner)
    send(edges.at[pl.ds(LEFT, 2)], edges.at[pl.ds(SIB, 2)], sib, R_EDGES)
    send(main, block.at[spot(part * PART, PART)], sib, R_MAIN)
    send(lroot_hbm.at[0], lroot.at[1], sib, R_LROOT, jnp.logical_not(early_roots))
    send(rroot_hbm.at[0], rroot.at[1], sib, R_RROOT, jnp.logical_not(early_roots))

    lines = lax.broadcasted_iota(jnp.int32, (EDGE, B), 0) * B + lax.broadcasted_iota(jnp.int32, (EDGE, B), 1)

    def merge(row, bound, slot, before):
        rows = spot(row, EDGE)
        here = block[rows, :].astype(jnp.float32)
        there = edges[slot].astype(jnp.float32)
        place = lines + row * B
        keep = place < bound if before else place >= bound
        block[rows, :] = jnp.where(keep, here, there).astype(jnp.bfloat16)

    pieces = (
        spot(other * PART, REST),
        spot(other * PART + PART + EDGE, REST),
        spot(other * PART + PART - EDGE, 2 * EDGE),
    )
    forwards = []

    def pass_on(there, prev_there, next_there):
        for i in range(2):
            arrived(block.at[pieces[i]], R_PART + i, there)
            forwards.append(send(block.at[pieces[i]], block.at[pieces[i]], sib, R_FWD + i, there))
        for i in range(2):
            rows = spot(other * PART + PART - EDGE + EDGE * i, EDGE)
            arrived(block.at[rows], R_SEAM + i, there)
        send(block.at[pieces[2]], block.at[pieces[2]], sib, R_FWD + 2, there)
        arrived(edges.at[ACROSS], R_ACROSS, there)
        arrived(edges.at[PREV], R_PREV, prev_there)
        arrived(edges.at[NEXT], R_NEXT, next_there)
        send(edges.at[pl.ds(PREV, 3)], edges.at[pl.ds(PREV, 3)], sib, R_FWD + 3, there)

    pass_on(takes_inner, jnp.logical_and(takes_inner, has_prev), jnp.logical_and(takes_inner, has_next))

    seam = 2 * chip * PART + PART
    seam_bound = seam * B + jnp.where(core == 0, next_shift, own_shift)
    arrived(edges.at[pl.ds(SIB, 2)], R_EDGES)
    arrived(block.at[spot(sib_part * PART, PART)], R_MAIN)
    merge(seam - EDGE, seam_bound, LEFT + SIB * (1 - core), True)
    merge(seam, seam_bound, RIGHT + SIB * core, False)
    seam_rows = spot(seam - EDGE + EDGE * core, EDGE)
    send(block.at[seam_rows], block.at[seam_rows], land, R_SEAM + core)

    load_owner.wait()
    owner_part = owner[me // 4] - base
    slot = jnp.where(owner_part == part, 0, 1)
    near = owner_part // 2 == chip
    owns = owner_part == part
    for copy in load_roots:
        copy.wait()
    arrived(lroot.at[1], R_LROOT, gives)
    arrived(rroot.at[1], R_RROOT, gives)

    @pl.when(gives_inner)
    def _():
        picked[...] = rroot[slot]

    @pl.when(gives_outer)
    def _():
        picked[pl.ds(0, THEIR_ROWS), :] = lroot[slot, pl.ds(0, THEIR_ROWS), :]

    send(picked, rtheirs, land, R_THEIRS, gives_inner)
    send(picked.at[pl.ds(0, THEIR_ROWS)], ltheirs, land, R_THEIRS + 1, gives_outer)

    bounds = [PART * B * j + shift_of(base + j) for j in (0, 2, 4)]

    pass_on(gets_inner, jnp.logical_and(gets_inner, has_prev), jnp.logical_and(gets_inner, has_next))
    for index in forwards:
        sent(index)
    for i in range(3):
        arrived(block.at[pieces[i]], R_FWD + i, is_outer)
    arrived(edges.at[pl.ds(PREV, 3)], R_FWD + 3, is_outer)

    merge(0, bounds[0], PREV, False)
    merge(2 * PART - EDGE, bounds[1], ACROSS - (ACROSS - SIB * core) * chip, True)
    merge(2 * PART, bounds[1], ACROSS - (ACROSS - RIGHT - SIB * (1 - core)) * (1 - chip), False)
    merge(4 * PART - EDGE, bounds[2], NEXT, True)

    arrived(lroot.at[1], R_LROOT, sends_rows)
    arrived(rroot.at[1], R_RROOT, sends_rows)

    def direction(*rows):
        lines = [lroot[slot, spot(row, size), :] for row, size in rows]
        left = lines[0] if len(lines) == 1 else jnp.concatenate(lines, axis=0)
        half = jnp.dot(left, block[...], preferred_element_type=jnp.float32).astype(jnp.bfloat16)
        return jnp.dot(half, rroot[slot], preferred_element_type=jnp.float32).astype(jnp.bfloat16)

    soon = (1 - chip) * (4 * PART - 2 * NEAR_ROWS + NEAR_ROWS * outer) + chip * NEAR_ROWS * inner
    last = (1 - chip) * (2 * PART - EDGE + LAST * outer) + chip * (2 * NEAR_ROWS + LAST * inner)

    @pl.when(is_inner)
    def _():
        ends = direction((0, EDGE), (4 * PART - EDGE, EDGE))
        head_out[0] = ends[:EDGE]
        head_out[1] = ends[EDGE:]

    send(head_out.at[0], head_in.at[chip], device(base - 1), R_HEAD + chip, inner_prev)
    send(head_out.at[1], head_in.at[chip], device(base + 4), R_HEAD + chip, inner_next)

    @pl.when(sends_rows)
    def _():
        pout[pl.ds(0, NEAR_ROWS), :] = direction((soon, NEAR_ROWS))

    send(pout.at[pl.ds(0, NEAR_ROWS)], pin.at[spot(soon, NEAR_ROWS)], land, R_SOON + core, sends_rows)

    @pl.when(sends_rows)
    def _():
        pout[pl.ds(NEAR_ROWS, LAST), :] = direction((last, LAST))

    send(pout.at[pl.ds(NEAR_ROWS, LAST)], pin.at[spot(last, LAST)], land, R_LAST + core, sends_rows)

    mine_at = part * PART - EDGE + EDGE * first - EDGE * final
    pown[...] = direction((mine_at, WROWS))

    for copy in load_facs:
        copy.wait()
    for dst, fac, dims in ((nl_out, lfac, (1, 1)), (nr_out, rfac, (0, 0))):
        for i in range(SPLIT):
            strip = pl.ds(i * LANES, LANES)
            one = block[strip, :] if dims[0] == 1 else block[:, strip]
            gram = lax.dot_general(
                one,
                block[...],
                (((dims[0],), (dims[1],)), ((), ())),
                preferred_element_type=jnp.float32,
            )
            fresh = 0.9 * fac[strip, :].astype(jnp.float32) + 0.1 * gram
            dst[0, strip, :] = jnp.where(owns, fresh, 0.0).astype(jnp.bfloat16)

    def sender_rows(whose):
        outer_there = (whose + chip) % 2
        near_at = chip * (4 * PART - 2 * NEAR_ROWS + NEAR_ROWS * outer_there) + (1 - chip) * NEAR_ROWS * (
            1 - outer_there
        )
        last_at = chip * (2 * PART - EDGE + LAST * outer_there) + (1 - chip) * (
            2 * NEAR_ROWS + LAST * (1 - outer_there)
        )
        return near_at, last_at

    for i in range(2):
        near_at, _ = sender_rows(i)
        arrived(pin.at[spot(near_at, NEAR_ROWS)], R_SOON + i, gets_inner)
    outer_rows = spot(chip * (4 * PART - OUTER_ROWS), OUTER_ROWS)
    send(pin.at[outer_rows], pin.at[outer_rows], sib, R_BACK, gets_inner)
    for i in range(2):
        _, last_at = sender_rows(i)
        arrived(pin.at[spot(last_at, LAST)], R_LAST + i, gets_inner)
    arrived(pin.at[outer_rows], R_BACK, gets_outer)
    def passed(ref, i):
        arrived(ref, R_THEIRS + i, takes_inner)
        send(ref, ref, sib, R_PASSED + i, takes_inner)
        arrived(ref, R_PASSED + i, takes_outer)

    their_rows = spot(part * (PART - EDGE), WROWS)
    passed(ltheirs, 1)

    @pl.when(takes)
    def _():
        halfway[...] = jnp.dot(
            ltheirs[their_rows, :], block[...], preferred_element_type=jnp.float32
        ).astype(jnp.bfloat16)

    passed(rtheirs, 0)

    @pl.when(takes)
    def _():
        pin[their_rows, :] = jnp.dot(
            halfway[...], rtheirs[...], preferred_element_type=jnp.float32
        ).astype(jnp.bfloat16)

    def mine(at, row, size):
        return jnp.where(
            near,
            pown[spot(at, size), :].astype(jnp.float32),
            pin[spot(row, size), :].astype(jnp.float32),
        )

    def place(row, value):
        for j in range(SPLIT):
            zwin[pl.ds(row * SPLIT + j, value.shape[0], stride=SPLIT), :] = pltpu.roll(
                value[:, j * LANES : (j + 1) * LANES], (LANES - along) % LANES, 1
            )

    place(EDGE, mine(EDGE - EDGE * first + EDGE * final, part * PART, PART))
    for i in range(2):
        arrived(head_in.at[i], R_HEAD + i, outer_beyond)
    beside = jnp.clip(me // 4 - 1 + 2 * chip, 0, owner.shape[0] - 1)
    head = jnp.where(
        (owner[beside] - 4 * beside) // 2 == 0,
        head_in[0].astype(jnp.float32),
        head_in[1].astype(jnp.float32),
    )
    top = mine(EDGE * final, part * PART - EDGE + EDGE * first, EDGE)
    place(0, jnp.where(part == 0, head, top))
    bottom = mine(EDGE + PART - EDGE * first, part * PART + PART - EDGE * final, EDGE)
    place(EDGE + PART, jnp.where(part == 3, head, bottom))

    lane = lax.broadcasted_iota(jnp.int32, (chunk, LANES), 1)
    flat = lax.broadcasted_iota(jnp.int32, (chunk, LANES), 0) * LANES + lane
    for i in range(8):
        at = i * chunk
        here = zwin[pl.ds(down + at, chunk), :]
        below = zwin[pl.ds(down + at + 1, chunk), :]
        value = jnp.where(lane + along < LANES, here, below)
        value = jnp.where(flat + at * LANES < length, value, 0.0)
        dir_out[pl.ds(at, chunk), :] = value.astype(jnp.bfloat16)

    for pair in sends:
        if pair is not None:
            only(pair[1], pair[0].wait_send)


def hand_over(*refs):
    sem = refs[-1]
    copies = [pltpu.make_async_copy(refs[i], refs[3 + i], sem.at[i]) for i in range(3)]
    for copy in copies:
        copy.start()
    for copy in copies:
        copy.wait()


def local(grad_shards, shard_length, block_owner, left_factor, right_factor, left_root, right_root):
    count = shard_length.shape[0]
    wide = LANES if count % LANES == 0 else count
    bf16 = jnp.bfloat16
    square = jax.ShapeDtypeStruct((1, B, B), bf16)
    call = pl.pallas_call(
        kernel,
        out_shape=(
            pltpu.VMEM((FLAT, LANES), bf16), pltpu.VMEM((1, B, B), bf16), pltpu.VMEM((1, B, B), bf16)
        ),
        in_specs=[pl.BlockSpec(memory_space=pl.ANY)] * 7,
        out_specs=[pl.BlockSpec(memory_space=pltpu.VMEM)] * 3,
        scratch_shapes=[
            pltpu.VMEM((count // wide, wide), jnp.int32),
            pltpu.SMEM(block_owner.shape, jnp.int32),
            pltpu.VMEM((FLAT, LANES), bf16),
            pltpu.VMEM((PAD + FLAT + 8, LANES), jnp.float32),
            pltpu.VMEM((7, EDGE, B), bf16),
            pltpu.VMEM((PART, B), bf16),
            pltpu.VMEM((B, B), bf16),
            pltpu.VMEM((2, B, B), bf16),
            pltpu.VMEM((2, B, B), bf16),
            pltpu.VMEM((B, B), bf16),
            pltpu.VMEM((THEIR_ROWS, B), bf16),
            pltpu.VMEM((B, B), bf16),
            pltpu.VMEM((B, B), bf16),
            pltpu.VMEM((B, B), bf16),
            pltpu.VMEM((NEAR_ROWS + LAST, B), bf16),
            pltpu.VMEM((WROWS, B), bf16),
            pltpu.VMEM((B, B), bf16),
            pltpu.VMEM((2, EDGE, B), bf16),
            pltpu.VMEM((2, EDGE, B), bf16),
            pltpu.VMEM((2, 16, LANES), bf16),
            pltpu.VMEM((WROWS, B), bf16),
            pltpu.VMEM((FLAT + PAD, LANES), jnp.float32),
            pltpu.SemaphoreType.DMA((7,)),
            pltpu.SemaphoreType.DMA((SENDS,)),
            pltpu.SemaphoreType.DMA((RECVS,)),
        ],
        compiler_params=pltpu.CompilerParams(
            collective_id=0, has_side_effects=True, vmem_limit_bytes=48 * 1024 * 1024
        ),
        name="shampoo_step",
    )
    given = (
        shard_length.reshape(count // wide, wide),
        block_owner,
        grad_shards.reshape(FLAT, LANES),
        left_factor,
        right_factor,
        left_root,
        right_root,
    )
    results = call(*(pltpu.with_memory_space_constraint(x, pltpu.HBM) for x in given))
    direction, new_left, new_right = pl.pallas_call(
        hand_over,
        out_shape=(jax.ShapeDtypeStruct((FLAT, LANES), bf16), square, square),
        in_specs=[pl.BlockSpec(memory_space=pltpu.VMEM)] * 3,
        out_specs=[pl.BlockSpec(memory_space=pl.ANY)] * 3,
        scratch_shapes=[pltpu.SemaphoreType.DMA((3,))],
        compiler_params=pltpu.CompilerParams(vmem_limit_bytes=16 * 1024 * 1024),
        name="hand_over",
    )(*(pltpu.with_memory_space_constraint(x, pltpu.VMEM) for x in results))
    return direction.reshape(grad_shards.shape), new_left, new_right


def solution(mesh):
    flat = P(("fsdp", "grp"))
    square = P(("fsdp", "grp"), None, None)
    return jax.shard_map(
        local,
        mesh=mesh,
        in_specs=(flat, P(), P(), square, square, square, square),
        out_specs=(flat, square, square),
        check_vma=False,
    )
```

```python
import functools

import jax
import jax.numpy as jnp
from jax import lax
from jax.experimental import pallas as pl
from jax.experimental.pallas import tpu as pltpu
from jax.sharding import PartitionSpec as P

B = 512
LANES = 128
PART = 128
EDGE = 32
WROWS = PART + 2 * EDGE
REST = PART - EDGE
FLAT = WROWS * B // LANES
SPLIT = B // LANES
PAD = 264
MESH = pl.DeviceIdType.MESH

NEAR_ROWS = 80
LAST = 64
OUTER_ROWS = 2 * NEAR_ROWS
THEIR_ROWS = 2 * PART + EDGE

LEFT, RIGHT, SIB, PREV, NEXT, ACROSS = 0, 1, 2, 4, 5, 6

(
    R_EDGES, R_MAIN, R_PART, R_SEAM, R_ACROSS, R_PREV, R_NEXT, R_FWD, R_LROOT, R_RROOT, R_SOON, R_LAST,
    R_BACK, R_HEAD, R_HELLO, R_THEIRS, R_PASSED, RECVS,
) = (0, 1, 2, 4, 6, 7, 8, 9, 13, 14, 15, 17, 19, 20, 22, 23, 25, 27)
SENDS = 30


def kernel(
    lens_hbm, owner_hbm, grad_hbm, lfac_hbm, rfac_hbm, lroot_hbm, rroot_hbm,
    dir_out, nl_out, nr_out,
    lens, owner, grad, shifted, edges, main, block, lroot, rroot, picked, ltheirs, rtheirs, lfac, rfac,
    pout, pown, pin, head_out, head_in, hello, halfway, zwin,
    in_sem, send_sem, recv_sem,
):
    f = lax.axis_index("fsdp")
    g = lax.axis_index("grp")
    nf = lax.axis_size("fsdp")
    ng = lax.axis_size("grp")
    me = f * ng + g
    part = g % 4
    core = g % 2
    chip = part // 2
    first = (3 - part) // 3
    final = part // 3
    outer = first + final
    inner = 1 - outer
    base = me - part
    has_prev = base > 0
    has_next = base + 4 < nf * ng
    is_outer = outer == 1
    is_inner = inner == 1
    gives = jnp.logical_and(base == 0, chip == 1)
    takes = jnp.logical_and(base == 0, chip == 0)
    sends_rows = jnp.logical_not(gives)
    gets_rows = jnp.logical_not(takes)
    greets_sib = jnp.logical_or(is_inner, gets_rows)
    early_roots = jnp.logical_and(is_outer, base == 0)
    gives_inner = jnp.logical_and(is_inner, gives)
    gives_outer = jnp.logical_and(is_outer, gives)
    takes_inner = jnp.logical_and(is_inner, takes)
    takes_outer = jnp.logical_and(is_outer, takes)
    gets_inner = jnp.logical_and(is_inner, gets_rows)
    gets_outer = jnp.logical_and(is_outer, gets_rows)
    beyond = jnp.logical_or(jnp.logical_and(chip == 0, has_prev), jnp.logical_and(chip == 1, has_next))
    outer_beyond = jnp.logical_and(is_outer, beyond)
    inner_prev = jnp.logical_and(is_inner, has_prev)
    inner_next = jnp.logical_and(is_inner, has_next)

    def device(index):
        index = index + ng
        return index // ng - 1, index % ng

    sib = (f, g + 1 - 2 * core)
    land = (f, g - part + 2 - chip)
    diag = (f, g - part + 3 - 3 * chip)
    sib_part = part + 1 - 2 * core
    other = 2 - 2 * chip

    def only(there, act):
        if there is None:
            act()
        else:
            pl.when(there)(act)

    def spot(start, size):
        return pl.ds(pl.multiple_of(start, 16), size)

    loads = []

    def load(src, dst):
        copy = pltpu.make_async_copy(src, dst, in_sem.at[len(loads)])
        copy.start()
        loads.append(copy)
        return copy

    sends = []

    def send(src, dst, to, arrival, there=None):
        copy = pltpu.make_async_remote_copy(
            src_ref=src,
            dst_ref=dst,
            send_sem=send_sem.at[len(sends)],
            recv_sem=recv_sem.at[arrival],
            device_id=to,
            device_id_type=MESH,
        )
        only(there, copy.start)
        sends.append((copy, there))
        return len(sends) - 1

    def sent(index):
        copy, there = sends[index]
        sends[index] = None
        only(there, copy.wait_send)

    def arrived(dst, arrival, here=None):
        copy = pltpu.make_async_remote_copy(
            src_ref=dst,
            dst_ref=dst,
            send_sem=send_sem.at[0],
            recv_sem=recv_sem.at[arrival],
            device_id=sib,
            device_id_type=MESH,
        )
        only(here, copy.wait_recv)

    load_grad = load(grad_hbm, grad)
    load_lens = load(lens_hbm, lens)

    barrier = pltpu.get_barrier_semaphore()
    for to, there in (
        (sib, greets_sib),
        (land, is_inner),
        (diag, is_inner),
        (device(base - 1), inner_prev),
        (device(base + 4), inner_next),
        (device(base - 3 + 8 * chip), outer_beyond),
        (device(base - 2 + 8 * chip), outer_beyond),
    ):
        only(there, functools.partial(pl.semaphore_signal, barrier, 1, device_id=to, device_id_type=MESH))
    greetings = inner * (1 + gets_rows.astype(jnp.int32) + has_prev.astype(jnp.int32) + has_next.astype(jnp.int32)) + outer * (
        2 + 2 * beyond.astype(jnp.int32)
    )

    def meet():
        pl.semaphore_wait(barrier, greetings)

    hello[0] = jnp.zeros(hello.shape[1:], hello.dtype)
    pl.when(is_outer)(meet)
    send(hello.at[0], hello.at[1], sib, R_HELLO, takes_outer)
    send(lroot_hbm.at[0], lroot.at[1], sib, R_LROOT, early_roots)
    send(rroot_hbm.at[0], rroot.at[1], sib, R_RROOT, early_roots)

    load_owner = load(owner_hbm, owner)
    load_roots = [load(lroot_hbm.at[0], lroot.at[0]), load(rroot_hbm.at[0], rroot.at[0])]
    load_facs = [load(lfac_hbm.at[0], lfac), load(rfac_hbm.at[0], rfac)]

    load_lens.wait()
    counts = lens[...] - PART * B
    spots = lax.broadcasted_iota(jnp.int32, counts.shape, 0) * counts.shape[1] + lax.broadcasted_iota(
        jnp.int32, counts.shape, 1
    )

    def shift_of(index):
        return jnp.sum(jnp.where(spots < index, counts, 0))

    own_shift = shift_of(me)
    next_shift = shift_of(me + 1)
    start = jnp.clip(own_shift + EDGE * B, 0, 2 * EDGE * B)
    length = next_shift - own_shift + PART * B
    down = start // LANES
    along = start % LANES

    load_grad.wait()
    chunk = FLAT // 8
    for i in range(8):
        at = i * chunk
        shifted[pl.ds(PAD + at, chunk), :] = pltpu.roll(
            grad[pl.ds(at, chunk), :].astype(jnp.float32), along, 1
        )

    def window(row, size, *dsts):
        lane = lax.broadcasted_iota(jnp.int32, (size, LANES), 1)
        for j in range(SPLIT):
            here = shifted[pl.ds(PAD - down + row * SPLIT + j, size, stride=SPLIT), :]
            above = shifted[pl.ds(PAD - 1 - down + row * SPLIT + j, size, stride=SPLIT), :]
            value = jnp.where(lane < along, above, here).astype(jnp.bfloat16)
            for dst in dsts:
                dst[:, pl.ds(j * LANES, LANES)] = value

    window(0, EDGE, edges.at[LEFT])
    window(WROWS - EDGE, EDGE, edges.at[RIGHT])
    window(EDGE, PART, main, block.at[spot(part * PART, PART)])

    pl.when(is_inner)(meet)

    rest = core * EDGE
    send(main.at[spot(rest, REST)], block.at[spot(part * PART + rest, REST)], land, R_PART + core)
    send(edges.at[1 - chip], edges.at[ACROSS], land, R_ACROSS, is_inner)
    for i in (1, 2):
        send(edges.at[chip], edges.at[NEXT - chip], device(base - 4 + 8 * chip + i), R_NEXT - chip, outer_beyond)
    arrived(hello.at[1], R_HELLO, takes_inner)
    send(edges.at[pl.ds(LEFT, 2)], edges.at[pl.ds(SIB, 2)], sib, R_EDGES)
    send(main, block.at[spot(part * PART, PART)], sib, R_MAIN)
    send(lroot_hbm.at[0], lroot.at[1], sib, R_LROOT, jnp.logical_not(early_roots))
    send(rroot_hbm.at[0], rroot.at[1], sib, R_RROOT, jnp.logical_not(early_roots))

    lines = lax.broadcasted_iota(jnp.int32, (EDGE, B), 0) * B + lax.broadcasted_iota(jnp.int32, (EDGE, B), 1)

    def merge(row, bound, slot, before):
        rows = spot(row, EDGE)
        here = block[rows, :].astype(jnp.float32)
        there = edges[slot].astype(jnp.float32)
        place = lines + row * B
        keep = place < bound if before else place >= bound
        block[rows, :] = jnp.where(keep, here, there).astype(jnp.bfloat16)

    pieces = (
        spot(other * PART, REST),
        spot(other * PART + PART + EDGE, REST),
        spot(other * PART + PART - EDGE, 2 * EDGE),
    )
    forwards = []

    def pass_on(there, prev_there, next_there):
        for i in range(2):
            arrived(block.at[pieces[i]], R_PART + i, there)
            forwards.append(send(block.at[pieces[i]], block.at[pieces[i]], sib, R_FWD + i, there))
        for i in range(2):
            rows = spot(other * PART + PART - EDGE + EDGE * i, EDGE)
            arrived(block.at[rows], R_SEAM + i, there)
        send(block.at[pieces[2]], block.at[pieces[2]], sib, R_FWD + 2, there)
        arrived(edges.at[ACROSS], R_ACROSS, there)
        arrived(edges.at[PREV], R_PREV, prev_there)
        arrived(edges.at[NEXT], R_NEXT, next_there)
        send(edges.at[pl.ds(PREV, 3)], edges.at[pl.ds(PREV, 3)], sib, R_FWD + 3, there)

    pass_on(takes_inner, jnp.logical_and(takes_inner, has_prev), jnp.logical_and(takes_inner, has_next))

    seam = 2 * chip * PART + PART
    seam_bound = seam * B + jnp.where(core == 0, next_shift, own_shift)
    arrived(edges.at[pl.ds(SIB, 2)], R_EDGES)
    arrived(block.at[spot(sib_part * PART, PART)], R_MAIN)
    merge(seam - EDGE, seam_bound, LEFT + SIB * (1 - core), True)
    merge(seam, seam_bound, RIGHT + SIB * core, False)
    seam_rows = spot(seam - EDGE + EDGE * core, EDGE)
    send(block.at[seam_rows], block.at[seam_rows], land, R_SEAM + core)

    load_owner.wait()
    owner_part = owner[me // 4] - base
    slot = jnp.where(owner_part == part, 0, 1)
    near = owner_part // 2 == chip
    owns = owner_part == part
    for copy in load_roots:
        copy.wait()
    arrived(lroot.at[1], R_LROOT, gives)
    arrived(rroot.at[1], R_RROOT, gives)

    @pl.when(gives_inner)
    def _():
        picked[...] = rroot[slot]

    @pl.when(gives_outer)
    def _():
        picked[pl.ds(0, THEIR_ROWS), :] = lroot[slot, pl.ds(0, THEIR_ROWS), :]

    send(picked, rtheirs, land, R_THEIRS, gives_inner)
    send(picked.at[pl.ds(0, THEIR_ROWS)], ltheirs, land, R_THEIRS + 1, gives_outer)

    bounds = [PART * B * j + shift_of(base + j) for j in (0, 2, 4)]

    pass_on(gets_inner, jnp.logical_and(gets_inner, has_prev), jnp.logical_and(gets_inner, has_next))
    for index in forwards:
        sent(index)
    for i in range(3):
        arrived(block.at[pieces[i]], R_FWD + i, is_outer)
    arrived(edges.at[pl.ds(PREV, 3)], R_FWD + 3, is_outer)

    merge(0, bounds[0], PREV, False)
    merge(2 * PART - EDGE, bounds[1], ACROSS - (ACROSS - SIB * core) * chip, True)
    merge(2 * PART, bounds[1], ACROSS - (ACROSS - RIGHT - SIB * (1 - core)) * (1 - chip), False)
    merge(4 * PART - EDGE, bounds[2], NEXT, True)

    arrived(lroot.at[1], R_LROOT, sends_rows)
    arrived(rroot.at[1], R_RROOT, sends_rows)

    def direction(*rows):
        lines = [lroot[slot, spot(row, size), :] for row, size in rows]
        left = lines[0] if len(lines) == 1 else jnp.concatenate(lines, axis=0)
        half = jnp.dot(left, block[...], preferred_element_type=jnp.float32).astype(jnp.bfloat16)
        return jnp.dot(half, rroot[slot], preferred_element_type=jnp.float32).astype(jnp.bfloat16)

    soon = (1 - chip) * (4 * PART - 2 * NEAR_ROWS + NEAR_ROWS * outer) + chip * NEAR_ROWS * inner
    last = (1 - chip) * (2 * PART - EDGE + LAST * outer) + chip * (2 * NEAR_ROWS + LAST * inner)

    @pl.when(is_inner)
    def _():
        ends = direction((0, EDGE), (4 * PART - EDGE, EDGE))
        head_out[0] = ends[:EDGE]
        head_out[1] = ends[EDGE:]

    send(head_out.at[0], head_in.at[chip], device(base - 1), R_HEAD + chip, inner_prev)
    send(head_out.at[1], head_in.at[chip], device(base + 4), R_HEAD + chip, inner_next)

    @pl.when(sends_rows)
    def _():
        pout[pl.ds(0, NEAR_ROWS), :] = direction((soon, NEAR_ROWS))

    send(pout.at[pl.ds(0, NEAR_ROWS)], pin.at[spot(soon, NEAR_ROWS)], land, R_SOON + core, sends_rows)

    @pl.when(sends_rows)
    def _():
        pout[pl.ds(NEAR_ROWS, LAST), :] = direction((last, LAST))

    send(pout.at[pl.ds(NEAR_ROWS, LAST)], pin.at[spot(last, LAST)], land, R_LAST + core, sends_rows)

    mine_at = part * PART - EDGE + EDGE * first - EDGE * final
    pown[...] = direction((mine_at, WROWS))

    for copy in load_facs:
        copy.wait()
    for dst, fac, dims in ((nl_out, lfac, (1, 1)), (nr_out, rfac, (0, 0))):
        for i in range(SPLIT):
            strip = pl.ds(i * LANES, LANES)
            one = block[strip, :] if dims[0] == 1 else block[:, strip]
            gram = lax.dot_general(
                one,
                block[...],
                (((dims[0],), (dims[1],)), ((), ())),
                preferred_element_type=jnp.float32,
            )
            fresh = 0.9 * fac[strip, :].astype(jnp.float32) + 0.1 * gram
            dst[0, strip, :] = jnp.where(owns, fresh, 0.0).astype(jnp.bfloat16)

    def sender_rows(whose):
        outer_there = (whose + chip) % 2
        near_at = chip * (4 * PART - 2 * NEAR_ROWS + NEAR_ROWS * outer_there) + (1 - chip) * NEAR_ROWS * (
            1 - outer_there
        )
        last_at = chip * (2 * PART - EDGE + LAST * outer_there) + (1 - chip) * (
            2 * NEAR_ROWS + LAST * (1 - outer_there)
        )
        return near_at, last_at

    for i in range(2):
        near_at, _ = sender_rows(i)
        arrived(pin.at[spot(near_at, NEAR_ROWS)], R_SOON + i, gets_inner)
    outer_rows = spot(chip * (4 * PART - OUTER_ROWS), OUTER_ROWS)
    send(pin.at[outer_rows], pin.at[outer_rows], sib, R_BACK, gets_inner)
    for i in range(2):
        _, last_at = sender_rows(i)
        arrived(pin.at[spot(last_at, LAST)], R_LAST + i, gets_inner)
    arrived(pin.at[outer_rows], R_BACK, gets_outer)
    def passed(ref, i):
        arrived(ref, R_THEIRS + i, takes_inner)
        send(ref, ref, sib, R_PASSED + i, takes_inner)
        arrived(ref, R_PASSED + i, takes_outer)

    their_rows = spot(part * (PART - EDGE), WROWS)
    passed(ltheirs, 1)

    @pl.when(takes)
    def _():
        halfway[...] = jnp.dot(
            ltheirs[their_rows, :], block[...], preferred_element_type=jnp.float32
        ).astype(jnp.bfloat16)

    passed(rtheirs, 0)

    @pl.when(takes)
    def _():
        pin[their_rows, :] = jnp.dot(
            halfway[...], rtheirs[...], preferred_element_type=jnp.float32
        ).astype(jnp.bfloat16)

    def mine(at, row, size):
        return jnp.where(
            near,
            pown[spot(at, size), :].astype(jnp.float32),
            pin[spot(row, size), :].astype(jnp.float32),
        )

    def place(row, value):
        for j in range(SPLIT):
            zwin[pl.ds(row * SPLIT + j, value.shape[0], stride=SPLIT), :] = pltpu.roll(
                value[:, j * LANES : (j + 1) * LANES], (LANES - along) % LANES, 1
            )

    place(EDGE, mine(EDGE - EDGE * first + EDGE * final, part * PART, PART))
    top = mine(EDGE * final, part * PART - EDGE + EDGE * first, EDGE)
    place(0, top)
    bottom = mine(EDGE + PART - EDGE * first, part * PART + PART - EDGE * final, EDGE)
    place(EDGE + PART, bottom)
    for i in range(2):
        arrived(head_in.at[i], R_HEAD + i, outer_beyond)
    beside = jnp.clip(me // 4 - 1 + 2 * chip, 0, owner.shape[0] - 1)
    head = jnp.where(
        (owner[beside] - 4 * beside) // 2 == 0,
        head_in[0].astype(jnp.float32),
        head_in[1].astype(jnp.float32),
    )

    @pl.when(part == 0)
    def _():
        place(0, head)

    @pl.when(part == 3)
    def _():
        place(EDGE + PART, head)

    lane = lax.broadcasted_iota(jnp.int32, (chunk, LANES), 1)
    flat = lax.broadcasted_iota(jnp.int32, (chunk, LANES), 0) * LANES + lane
    for i in range(8):
        at = i * chunk
        here = zwin[pl.ds(down + at, chunk), :]
        below = zwin[pl.ds(down + at + 1, chunk), :]
        value = jnp.where(lane + along < LANES, here, below)
        value = jnp.where(flat + at * LANES < length, value, 0.0)
        dir_out[pl.ds(at, chunk), :] = value.astype(jnp.bfloat16)

    for pair in sends:
        if pair is not None:
            only(pair[1], pair[0].wait_send)


def hand_over(*refs):
    sem = refs[-1]
    copies = [pltpu.make_async_copy(refs[i], refs[3 + i], sem.at[i]) for i in range(3)]
    for copy in copies:
        copy.start()
    for copy in copies:
        copy.wait()


def local(grad_shards, shard_length, block_owner, left_factor, right_factor, left_root, right_root):
    count = shard_length.shape[0]
    wide = LANES if count % LANES == 0 else count
    bf16 = jnp.bfloat16
    square = jax.ShapeDtypeStruct((1, B, B), bf16)
    call = pl.pallas_call(
        kernel,
        out_shape=(
            pltpu.VMEM((FLAT, LANES), bf16), pltpu.VMEM((1, B, B), bf16), pltpu.VMEM((1, B, B), bf16)
        ),
        in_specs=[pl.BlockSpec(memory_space=pl.ANY)] * 7,
        out_specs=[pl.BlockSpec(memory_space=pltpu.VMEM)] * 3,
        scratch_shapes=[
            pltpu.VMEM((count // wide, wide), jnp.int32),
            pltpu.SMEM(block_owner.shape, jnp.int32),
            pltpu.VMEM((FLAT, LANES), bf16),
            pltpu.VMEM((PAD + FLAT + 8, LANES), jnp.float32),
            pltpu.VMEM((7, EDGE, B), bf16),
            pltpu.VMEM((PART, B), bf16),
            pltpu.VMEM((B, B), bf16),
            pltpu.VMEM((2, B, B), bf16),
            pltpu.VMEM((2, B, B), bf16),
            pltpu.VMEM((B, B), bf16),
            pltpu.VMEM((THEIR_ROWS, B), bf16),
            pltpu.VMEM((B, B), bf16),
            pltpu.VMEM((B, B), bf16),
            pltpu.VMEM((B, B), bf16),
            pltpu.VMEM((NEAR_ROWS + LAST, B), bf16),
            pltpu.VMEM((WROWS, B), bf16),
            pltpu.VMEM((B, B), bf16),
            pltpu.VMEM((2, EDGE, B), bf16),
            pltpu.VMEM((2, EDGE, B), bf16),
            pltpu.VMEM((2, 16, LANES), bf16),
            pltpu.VMEM((WROWS, B), bf16),
            pltpu.VMEM((FLAT + PAD, LANES), jnp.float32),
            pltpu.SemaphoreType.DMA((7,)),
            pltpu.SemaphoreType.DMA((SENDS,)),
            pltpu.SemaphoreType.DMA((RECVS,)),
        ],
        compiler_params=pltpu.CompilerParams(
            collective_id=0, has_side_effects=True, vmem_limit_bytes=48 * 1024 * 1024
        ),
        name="shampoo_step",
    )
    given = (
        shard_length.reshape(count // wide, wide),
        block_owner,
        grad_shards.reshape(FLAT, LANES),
        left_factor,
        right_factor,
        left_root,
        right_root,
    )
    results = call(*(pltpu.with_memory_space_constraint(x, pltpu.HBM) for x in given))
    direction, new_left, new_right = pl.pallas_call(
        hand_over,
        out_shape=(jax.ShapeDtypeStruct((FLAT, LANES), bf16), square, square),
        in_specs=[pl.BlockSpec(memory_space=pltpu.VMEM)] * 3,
        out_specs=[pl.BlockSpec(memory_space=pl.ANY)] * 3,
        scratch_shapes=[pltpu.SemaphoreType.DMA((3,))],
        compiler_params=pltpu.CompilerParams(vmem_limit_bytes=16 * 1024 * 1024),
        name="hand_over",
    )(*(pltpu.with_memory_space_constraint(x, pltpu.VMEM) for x in results))
    return direction.reshape(grad_shards.shape), new_left, new_right


def solution(mesh):
    flat = P(("fsdp", "grp"))
    square = P(("fsdp", "grp"), None, None)
    return jax.shard_map(
        local,
        mesh=mesh,
        in_specs=(flat, P(), P(), square, square, square, square),
        out_specs=(flat, square, square),
        check_vma=False,
    )
```
